32 devices in a mesh: groups: 2 (over y), row: 4 (over x, core), col: 4 (over z).
Axes of the slice: x: 2, y: 2, z: 4, core: 2. Of those that a mesh axis runs over, the one named last changes fastest.
Arguments:
- shear_stress: float32 [8192, 512], P(('groups', 'row', 'col')), parts along dimension 0, may hold values from -0.3 to 0.3
- slip_state: float32 [8192, 512], P(('groups', 'row', 'col')), parts along dimension 0, may hold values from -0.15 to 0.15
- friction_a: float32 [8192, 512], P(('groups', 'row', 'col')), parts along dimension 0, may hold values from 0.15 to 0.3
- friction_b: float32 [8192, 512], P(('groups', 'row', 'col')), parts along dimension 0, may hold values from 0.1 to 0.4
- kernel: bfloat16 [8192, 4096], P(('groups', 'row'), 'col'), parts along dimension 0
- left_factors: bfloat16 [32, 16, 32, 256], P(('groups', 'row'), 'col'), parts along dimension 0, may hold values from -0.25 to 0.25
- right_factors: bfloat16 [32, 16, 32, 256], P(('groups', 'row'), 'col'), parts along dimension 0, may hold values from -0.375 to 0.375
- admissible: int32 [32, 16], P(('groups', 'row'), 'col'), parts along dimension 0, may hold values from 0 to 1, as said below
- ranks: int32 [32, 16], P(('groups', 'row'), 'col'), parts along dimension 0, may hold values from 1 to 32
Outputs:
- new_stress: float32 [8192, 512], P(('groups', 'row', 'col')), parts along dimension 0
- new_state: float32 [8192, 512], P(('groups', 'row', 'col')), parts along dimension 0
- mean_rate: float32 [8192, 512], P(('groups', 'row', 'col')), parts along dimension 0
The draws below stay inside these ranges and needn't reach their ends.
There are 2 independent parts, one for each index of `groups`. The reference program is written for one: setup_inputs(seed, part) draws one part's arguments, and reference() takes and returns one part's arrays. A program takes and returns all parts, laid end to end along the dimension named above; each array names one. Nothing has to cross between parts.
Inputs may be any that keep to these rules, and one draw needn't show every extreme that they name: `admissible`: the sub-block that couples each patch with itself is dense.
All inputs are finite; a program needn't handle non-finite values.
Results may differ from the reference program's by a relative error of at most 0.0055.
Values may be sent and summed in bfloat16 or wider, within the bound.
A program may use at most 64 MiB of HBM per device.

```python
import math
import jax
import jax.numpy as jnp
from jax import lax

SUB = 256
SUB_DEV = 4
RMAX = 32
ENS = 512
PATCH_DEV = 1024
QDEV = 256
NPATCH = 4096
GRID = 16
GRIDC = 16
N_ROW = 4
N_COL = 4


def draw_kernel(key, part):
    key = jax.random.fold_in(key, 11)
    grid_shape = (NPATCH, NPATCH)
    values = jax.random.normal(key, grid_shape, jnp.float32)
    values = values / math.sqrt(NPATCH)
    patch_index = jnp.arange(NPATCH, dtype=jnp.int32)
    self_column = patch_index % PATCH_DEV // QDEV * PATCH_DEV + patch_index // PATCH_DEV * QDEV + patch_index % QDEV
    values = values.at[patch_index, self_column].add(1.0)
    return values.astype(jnp.bfloat16)


def draw_admissible(key, part):
    key = jax.random.fold_in(key, 23)
    row_index = lax.broadcasted_iota(jnp.int32, (GRID, GRIDC), 0)
    col_index = lax.broadcasted_iota(jnp.int32, (GRID, GRIDC), 1)
    dev_row = row_index // SUB_DEV
    dev_col = col_index // SUB_DEV
    apart = jnp.abs(dev_row - dev_col)
    apart = jnp.minimum(apart, N_ROW - apart)
    dice = jax.random.randint(key, (GRID, GRIDC), 0, 8)
    near_field = dice < jnp.maximum(1, 6 - 2 * apart)
    own_block = (row_index % SUB_DEV == dev_col * QDEV // SUB) & (col_index % SUB_DEV == dev_row * QDEV // SUB)
    return jnp.where(near_field | own_block, 0, 1).astype(jnp.int32)


def touch_ends(drawn, own_key, least, high):
    shape = drawn.shape
    place = [jax.random.randint(jax.random.fold_in(own_key, axis), (), 0, shape[axis]) for axis in range(len(shape))]
    drawn = drawn.at[tuple(place)].set(least)
    longest = shape.index(max(shape))
    place[longest] = (place[longest] + 1) % shape[longest]
    return drawn.at[tuple(place)].set(high)


def shard_levels(own_key, shape, shards, low, high):
    factor_of = 1.0
    for position, parts in shards:
        steps = jax.random.uniform(jax.random.fold_in(jax.random.fold_in(own_key, 6), position), (parts,), jnp.float32, low / len(shards), high / len(shards))
        factor_of = factor_of * jnp.repeat(jnp.exp(steps), shape[position] // parts).reshape((-1,) + (1,) * (len(shape) - 1 - position))
    return factor_of


def bell_draw(key, extent, scale, bound, split=(), kind=jnp.bfloat16):
    values = jax.random.normal(key, extent, jnp.float32) * scale
    if len(split) > 0:
        values = shard_levels(key, extent, split, -0.22, 0.18) * values
    return jnp.clip(values, min=-bound, max=bound).astype(kind)


def setup_inputs(seed: int = 0, part: int = 0) -> dict:
    seeds = jax.random.split(jax.random.key(seed), 10)
    part_splits = jax.random.split(jax.random.fold_in(seeds[9], part), 10)
    shear_stress = jnp.clip(jax.random.uniform(part_splits[0], (NPATCH, ENS), jnp.float32, -0.3, 0.3) * shard_levels(part_splits[0], (NPATCH, ENS), ((0, 16),), -0.4, 0.0), -0.3, 0.3)
    slip_state = jnp.clip(jax.random.uniform(part_splits[1], (NPATCH, ENS), jnp.float32, -0.15, 0.15) * shard_levels(part_splits[1], (NPATCH, ENS), ((0, 16),), -0.4, 0.0), -0.15, 0.15)
    friction_a = jnp.clip(jnp.exp(math.log(0.3) - 0.6931472 * jax.random.uniform(part_splits[2], (NPATCH, ENS), jnp.float32) ** shard_levels(part_splits[2], (NPATCH, ENS), ((0, 16),), -0.2, 0.2)), 0.15, 0.3)
    friction_b = jnp.clip(jnp.exp(math.log(0.4) - 1.3862944 * jax.random.uniform(part_splits[3], (NPATCH, ENS), jnp.float32) ** shard_levels(part_splits[3], (NPATCH, ENS), ((0, 16),), -0.2, 0.2)), 0.1, 0.4)
    kernel = draw_kernel(jax.random.fold_in(jax.random.fold_in(seeds[9], part), 71), part)
    left_factors = bell_draw(part_splits[5], (GRID, GRIDC, RMAX, SUB), (RMAX * GRIDC) ** -0.5, 0.25, ((0, 4), (1, 4)))
    right_factors = bell_draw(part_splits[6], (GRID, GRIDC, RMAX, SUB), SUB ** -0.5, 0.375, ((0, 4), (1, 4)))
    admissible = draw_admissible(jax.random.fold_in(jax.random.fold_in(seeds[9], part), 71), part)
    ranks = touch_ends(jax.random.randint(part_splits[8], (GRID, GRIDC), 1, RMAX + 1), jax.random.fold_in(part_splits[8], 1), 1, RMAX).astype(jnp.int32)
    return dict(shear_stress=shear_stress, slip_state=slip_state, friction_a=friction_a, friction_b=friction_b, kernel=kernel, left_factors=left_factors, right_factors=right_factors, admissible=admissible, ranks=ranks)


time_step = 0.005


def slip_speed(stress, state_now, friction_a):
    return 2.0 * jnp.sinh(stress / friction_a) * jnp.exp(-state_now / friction_a)


def block_stress(deficit, kernel, left_factors, right_factors, admissible, ranks):
    slip_cols = deficit.astype(jnp.float32).reshape(N_ROW, N_COL, QDEV, ENS)
    slip_cols = slip_cols.transpose(1, 0, 2, 3).reshape(N_COL, PATCH_DEV, ENS)
    slip_subs = slip_cols.reshape(GRIDC, SUB, ENS)
    rank_index = jnp.arange(RMAX, dtype=jnp.int32)
    live_all = ((rank_index[None, None, :] < ranks[:, :, None]) & (admissible[:, :, None] == 1)).astype(jnp.float32)

    def row_block(blk):
        offset = (blk * PATCH_DEV).astype(jnp.int32)
        sub_offset = (blk * SUB_DEV).astype(jnp.int32)
        row_slab = lax.dynamic_slice_in_dim(kernel, offset, PATCH_DEV, 0).astype(jnp.float32)
        dense_flag = lax.dynamic_slice_in_dim(admissible, sub_offset, SUB_DEV, 0) == 0
        near_tile = jnp.where(dense_flag[:, None, :, None], row_slab.reshape(SUB_DEV, SUB, GRIDC, SUB), 0.0)
        near_tile = near_tile.reshape(PATCH_DEV, N_COL, PATCH_DEV)
        near_part = jnp.einsum("pcq,cqe->cpe", near_tile, slip_cols, precision=lax.Precision.HIGHEST)
        right_rows = lax.dynamic_slice_in_dim(right_factors, sub_offset, SUB_DEV, 0).astype(jnp.float32)
        left_rows = lax.dynamic_slice_in_dim(left_factors, sub_offset, SUB_DEV, 0).astype(jnp.float32)
        live_rank = lax.dynamic_slice_in_dim(live_all, sub_offset, SUB_DEV, 0)
        coefficients = jnp.einsum("ijrb,jbe->ijre", right_rows, slip_subs, precision=lax.Precision.HIGHEST)
        coefficients = coefficients * live_rank[..., None]
        coefficients = lax.optimization_barrier(coefficients.astype(jnp.bfloat16)).astype(jnp.float32)
        far_part = jnp.einsum("ijrb,ijre->jibe", left_rows, coefficients, precision=lax.Precision.HIGHEST)
        far_part = far_part.reshape(N_COL, SUB_DEV, SUB_DEV, SUB, ENS).sum(axis=1).reshape(N_COL, PATCH_DEV, ENS)
        partial_value = lax.optimization_barrier((near_part + far_part).astype(jnp.bfloat16)).astype(jnp.float32)
        return jnp.sum(partial_value, axis=0)

    stacked = lax.map(row_block, jnp.arange(N_ROW, dtype=jnp.int32))
    return stacked.reshape(NPATCH, ENS)


def reference(shear_stress, slip_state, friction_a, friction_b, kernel, left_factors, right_factors, admissible, ranks):
    def friction_rates(stress, state_now):
        speed_now = slip_speed(stress, state_now, friction_a)
        deficit = (1.0 - speed_now).astype(jnp.bfloat16)
        stress_rate = block_stress(deficit, kernel, left_factors, right_factors, admissible, ranks)
        state_rate = friction_b * (jnp.exp(-state_now / friction_b) - speed_now)
        return stress_rate, state_rate

    first_stress, first_state = friction_rates(shear_stress, slip_state)
    mid_stress = shear_stress + time_step * first_stress
    mid_state = slip_state + time_step * first_state
    second_stress, second_state = friction_rates(mid_stress, mid_state)
    mean_rate = 0.5 * (first_stress + second_stress)
    new_stress = shear_stress + time_step * mean_rate
    new_state = slip_state + 0.5 * time_step * (first_state + second_state)
    return new_stress, new_state, mean_rate
```

```python
import functools

import jax
import jax.numpy as jnp
from jax import lax
from jax.experimental import pallas as pl
from jax.experimental.pallas import tpu as pltpu
from jax.sharding import PartitionSpec as P

time_step = 0.005
LANES = 128
LAG_FORWARD = 1
LAG_FINAL = 2
MESH = pl.DeviceIdType.MESH
F32 = jnp.float32
BF16 = jnp.bfloat16


def step_kernel(
    n_row,
    n_col,
    shear_hbm,
    slip_hbm,
    fa_hbm,
    fb_hbm,
    kernel_hbm,
    left_hbm,
    right_hbm,
    admissible,
    ranks,
    stress_hbm,
    state_hbm,
    mean_hbm,
    s0,
    v0,
    fa,
    fb,
    kern,
    left,
    right,
    dense,
    state_rate,
    first_stress,
    first_state,
    total,
    slip_all,
    part,
    from_low,
    from_high,
    out_stress,
    out_state,
    out_mean,
    in_sem,
    op_sem,
    out_sem,
    gather_send,
    gather_recv,
    up_send,
    up_recv,
    down_send,
    down_recv,
):
    row = lax.axis_index("row")
    col = lax.axis_index("col")
    chunks, q = s0.shape[0], s0.shape[1]
    steps = 2 * chunks
    subs = admissible.shape[0]
    sub = left.shape[3]
    rank_max = left.shape[2]
    lower_half = col < n_col // 2

    def load(which, e):
        src = (shear_hbm, slip_hbm, fa_hbm, fb_hbm)[which]
        dst = (s0, v0, fa, fb)[which]
        return pltpu.make_async_copy(
            src.at[:, pl.ds(e * LANES, LANES)], dst.at[e], in_sem.at[which, e]
        )

    def load_op(which):
        src = (kernel_hbm, left_hbm, right_hbm)[which]
        dst = (kern, left, right)[which]
        return pltpu.make_async_copy(src, dst, op_sem.at[which])

    barrier = pltpu.get_barrier_semaphore()
    for k in range(1, n_row):
        pl.semaphore_signal(
            barrier, inc=1, device_id={"row": lax.rem(row + k, n_row)}, device_id_type=MESH
        )

    @pl.when(col > 0)
    def _():
        pl.semaphore_signal(barrier, inc=1, device_id={"col": col - 1}, device_id_type=MESH)

    @pl.when(col < n_col - 1)
    def _():
        pl.semaphore_signal(barrier, inc=1, device_id={"col": col + 1}, device_id_type=MESH)

    for e in range(chunks):
        for which in range(4):
            load(which, e).start()
        if e == 0:
            for which in range(3):
                load_op(which).start()

    def deficit_step(sec, e, stress, state):
        a, b = fa[e], fb[e]
        inv_a = 1.0 / a
        speed = jnp.exp((stress - state) * inv_a) - jnp.exp((-stress - state) * inv_a)
        slip_all[sec, e, pl.ds(pl.multiple_of(row * q, q), q), :] = (1.0 - speed).astype(BF16)
        state_rate[sec, e] = b * (jnp.exp(-state / b) - speed)

    def gather_copy(sec, e, k):
        block = slip_all.at[sec, e, pl.ds(pl.multiple_of(row * q, q), q), :]
        return pltpu.make_async_remote_copy(
            src_ref=block,
            dst_ref=block,
            send_sem=gather_send.at[sec, e, k - 1],
            recv_sem=gather_recv.at[sec, e, k - 1],
            device_id={"row": lax.rem(row + k, n_row)},
            device_id_type=MESH,
        )

    def start_gather(sec, e):
        for k in range(1, n_row):
            gather_copy(sec, e, k).start()

    def up_copy(sec, e, d):
        return pltpu.make_async_remote_copy(
            src_ref=part.at[sec, e, d],
            dst_ref=from_low.at[sec, e, d],
            send_sem=up_send.at[sec, e, d],
            recv_sem=up_recv.at[sec, e, d],
            device_id={"col": col + 1},
            device_id_type=MESH,
        )

    def down_copy(sec, e, d):
        return pltpu.make_async_remote_copy(
            src_ref=part.at[sec, e, d],
            dst_ref=from_high.at[sec, e, d],
            send_sem=down_send.at[sec, e, d],
            recv_sem=down_recv.at[sec, e, d],
            device_id={"col": col - 1},
            device_id_type=MESH,
        )

    def target(i):
        return jnp.where(lower_half, n_col - 1 - i, i)

    for which in range(4):
        load(which, 0).wait()
    deficit_step(0, 0, s0[0], v0[0])

    below, above = jnp.minimum(col, 1), jnp.minimum(n_col - 1 - col, 1)
    pl.semaphore_wait(barrier, n_row - 1 + below + above)

    start_gather(0, 0)

    @pl.loop(1, chunks)
    def _(e):
        for which in range(4):
            load(which, e).wait()
        deficit_step(0, e, s0[e], v0[e])
        start_gather(0, e)

    for which in range(3):
        load_op(which).wait()

    rank_at = lax.broadcasted_iota(jnp.int32, (rank_max, sub), 0)
    lane_at = lax.broadcasted_iota(jnp.int32, (sub, sub), 1)

    @pl.loop(0, subs)
    def _(i):
        rows = pl.ds(pl.multiple_of(i * sub, sub), sub)
        for j in range(subs):
            far = admissible[i, j]
            live = rank_at < far * ranks[i, j]
            factor = jnp.where(live, left[i, j].astype(F32), 0.0).astype(BF16)
            low = lax.dot_general(
                factor, right[i, j], (((0,), (0,)), ((), ())), preferred_element_type=F32
            )
            near = jnp.where(
                lane_at >= far * sub, kern[rows, pl.ds(j * sub, sub)].astype(F32), low
            )
            dense[rows, pl.ds(j * sub, sub)] = near.astype(BF16)

    def multiply(sec, e):
        for k in range(1, n_row):
            gather_copy(sec, e, k).wait_recv()
        slips = slip_all[sec, e]

        @pl.loop(0, n_col)
        def _(i):
            d = target(i)
            rows = pl.ds(pl.multiple_of(d * q, q), q)
            part[sec, e, d] = jnp.dot(
                dense[rows, :], slips, preferred_element_type=F32
            ).astype(BF16)

            @pl.when((col == 0) & (d > 0))
            def _():
                up_copy(sec, e, d).start()

            @pl.when((col == n_col - 1) & (d < col))
            def _():
                down_copy(sec, e, d).start()

    def forward(sec, e):
        @pl.loop(0, n_col)
        def _(i):
            d = target(i)

            @pl.when((col > 0) & (d > col))
            def _():
                up_copy(sec, e, d).wait_recv()
                part[sec, e, d] = (
                    part[sec, e, d].astype(F32) + from_low[sec, e, d].astype(F32)
                ).astype(BF16)
                up_copy(sec, e, d).start()

            @pl.when((col < n_col - 1) & (d < col))
            def _():
                down_copy(sec, e, d).wait_recv()
                part[sec, e, d] = (
                    part[sec, e, d].astype(F32) + from_high[sec, e, d].astype(F32)
                ).astype(BF16)
                down_copy(sec, e, d).start()

    def store(which, e):
        src = (out_stress, out_state, out_mean)[which]
        dst = (stress_hbm, state_hbm, mean_hbm)[which]
        return pltpu.make_async_copy(
            src.at[e], dst.at[:, pl.ds(e * LANES, LANES)], out_sem.at[which, e]
        )

    def finish(sec, e):
        total[...] = part[sec, e, col].astype(F32)

        @pl.when(col > 0)
        def _():
            up_copy(sec, e, col).wait_recv()
            total[...] += from_low[sec, e, col].astype(F32)

        @pl.when(col < n_col - 1)
        def _():
            down_copy(sec, e, col).wait_recv()
            total[...] += from_high[sec, e, col].astype(F32)

        @pl.when(sec == 0)
        def _():
            rate = total[...]
            first_stress[e] = rate
            deficit_step(
                1, e, s0[e] + time_step * rate, v0[e] + time_step * state_rate[0, e]
            )
            start_gather(1, e)

        @pl.when(sec == 1)
        def _():
            mean = 0.5 * (first_stress[e] + total[...])
            out_mean[e] = mean
            out_stress[e] = s0[e] + time_step * mean
            out_state[e] = v0[e] + 0.5 * time_step * (state_rate[0, e] + state_rate[1, e])
            for which in range(3):
                store(which, e).start()

    @pl.loop(0, steps + LAG_FINAL)
    def _(t):
        @pl.when(t < steps)
        def _():
            multiply(t // chunks, lax.rem(t, chunks))

        u = t - LAG_FORWARD

        @pl.when((u >= 0) & (u < steps))
        def _():
            forward(u // chunks, lax.rem(u, chunks))

        w = t - LAG_FINAL

        @pl.when(w >= 0)
        def _():
            finish(w // chunks, lax.rem(w, chunks))

    @pl.loop(0, steps)
    def _(t):
        sec, e = t // chunks, lax.rem(t, chunks)
        for k in range(1, n_row):
            gather_copy(sec, e, k).wait_send()

        @pl.loop(0, n_col)
        def _(d):
            @pl.when(d > col)
            def _():
                up_copy(sec, e, d).wait_send()

            @pl.when(d < col)
            def _():
                down_copy(sec, e, d).wait_send()

    @pl.loop(0, chunks)
    def _(e):
        for which in range(3):
            store(which, e).wait()


def per_device(
    n_row,
    n_col,
    shear_stress,
    slip_state,
    friction_a,
    friction_b,
    kernel,
    left_factors,
    right_factors,
    admissible,
    ranks,
):
    q, members = shear_stress.shape
    block = kernel.shape[0]
    chunks = members // LANES
    field = pltpu.VMEM((chunks, q, LANES), F32)
    sem = pltpu.SemaphoreType.DMA
    anywhere = pl.BlockSpec(memory_space=pl.ANY)
    scalars = pl.BlockSpec(memory_space=pltpu.SMEM)
    out = jax.ShapeDtypeStruct((q, members), F32)
    return tuple(
        pl.pallas_call(
            functools.partial(step_kernel, n_row, n_col),
            out_shape=(out, out, out),
            in_specs=[anywhere] * 7 + [scalars] * 2,
            out_specs=(anywhere,) * 3,
            scratch_shapes=[
                field,
                field,
                field,
                field,
                pltpu.VMEM(kernel.shape, BF16),
                pltpu.VMEM(left_factors.shape, BF16),
                pltpu.VMEM(right_factors.shape, BF16),
                pltpu.VMEM(kernel.shape, BF16),
                pltpu.VMEM((2, chunks, q, LANES), F32),
                field,
                field,
                pltpu.VMEM((q, LANES), F32),
                pltpu.VMEM((2, chunks, n_row * q, LANES), BF16),
                pltpu.VMEM((2, chunks, n_col, q, LANES), BF16),
                pltpu.VMEM((2, chunks, n_col, q, LANES), BF16),
                pltpu.VMEM((2, chunks, n_col, q, LANES), BF16),
                field,
                field,
                field,
                sem((4, chunks)),
                sem((3,)),
                sem((3, chunks)),
                sem((2, chunks, n_row - 1)),
                sem((2, chunks, n_row - 1)),
                sem((2, chunks, n_col)),
                sem((2, chunks, n_col)),
                sem((2, chunks, n_col)),
                sem((2, chunks, n_col)),
            ],
            compiler_params=pltpu.CompilerParams(
                collective_id=0, has_side_effects=True, vmem_limit_bytes=48 * 1024 * 1024
            ),
            cost_estimate=pl.CostEstimate(
                flops=4 * block * block * members,
                bytes_accessed=7 * 4 * q * members + 2 * block * block,
                transcendentals=8 * q * members,
            ),
        )(
            shear_stress,
            slip_state,
            friction_a,
            friction_b,
            kernel,
            left_factors,
            right_factors,
            admissible,
            ranks,
        )
    )


def solution(mesh):
    vector = P(("groups", "row", "col"), None)
    return jax.shard_map(
        functools.partial(per_device, mesh.shape["row"], mesh.shape["col"]),
        mesh=mesh,
        in_specs=(
            vector,
            vector,
            vector,
            vector,
            P(("groups", "row"), "col"),
            P(("groups", "row"), "col", None, None),
            P(("groups", "row"), "col", None, None),
            P(("groups", "row"), "col"),
            P(("groups", "row"), "col"),
        ),
        out_specs=(vector, vector, vector),
        check_vma=False,
    )
```

```python
import functools

import jax
import jax.numpy as jnp
from jax import lax
from jax.experimental import pallas as pl
from jax.experimental.pallas import tpu as pltpu
from jax.sharding import PartitionSpec as P

time_step = 0.005
LANES = 128
LAG_FORWARD = 1
LAG_FINAL = 2
MESH = pl.DeviceIdType.MESH
F32 = jnp.float32
BF16 = jnp.bfloat16


def step_kernel(
    n_row,
    n_col,
    shear_hbm,
    slip_hbm,
    fa_hbm,
    fb_hbm,
    kernel_hbm,
    left_hbm,
    right_hbm,
    admissible,
    ranks,
    stress_hbm,
    state_hbm,
    mean_hbm,
    s0,
    v0,
    fa,
    fb,
    kern,
    left,
    right,
    dense,
    state_rate,
    first_stress,
    first_state,
    total,
    slip_all,
    part,
    relay,
    inbox,
    out_stress,
    out_state,
    out_mean,
    in_sem,
    op_sem,
    out_sem,
    gather_send,
    gather_recv,
    relay_send,
    relay_recv,
    inbox_send,
    inbox_recv,
):
    row = lax.axis_index("row")
    col = lax.axis_index("col")
    chunks, q = s0.shape[0], s0.shape[1]
    steps = 2 * chunks
    subs = admissible.shape[0]
    sub = left.shape[3]
    rank_max = left.shape[2]
    lower_half = col < n_col // 2
    at_end = (col == 0) | (col == n_col - 1)
    beside_end = (col == 1) | (col == n_col - 2)
    end = jnp.where(lower_half, 0, n_col - 1)

    def load(which, e):
        src = (shear_hbm, slip_hbm, fa_hbm, fb_hbm)[which]
        dst = (s0, v0, fa, fb)[which]
        return pltpu.make_async_copy(
            src.at[:, pl.ds(e * LANES, LANES)], dst.at[e], in_sem.at[which, e]
        )

    def load_op(which):
        src = (kernel_hbm, left_hbm, right_hbm)[which]
        dst = (kern, left, right)[which]
        return pltpu.make_async_copy(src, dst, op_sem.at[which])

    barrier = pltpu.get_barrier_semaphore()
    for k in range(1, n_row):
        pl.semaphore_signal(
            barrier, inc=1, device_id={"row": lax.rem(row + k, n_row)}, device_id_type=MESH
        )

    for k in range(1, n_col):
        pl.semaphore_signal(
            barrier, inc=1, device_id={"col": lax.rem(col + k, n_col)}, device_id_type=MESH
        )

    for e in range(chunks):
        for which in range(4):
            load(which, e).start()
        if e == 0:
            for which in range(3):
                load_op(which).start()

    def deficit_step(sec, e, stress, state):
        a, b = fa[e], fb[e]
        inv_a = 1.0 / a
        speed = jnp.exp((stress - state) * inv_a) - jnp.exp((-stress - state) * inv_a)
        slip_all[sec, e, pl.ds(pl.multiple_of(row * q, q), q), :] = (1.0 - speed).astype(BF16)
        state_rate[sec, e] = b * (jnp.exp(-state / b) - speed)

    def gather_copy(sec, e, k):
        block = slip_all.at[sec, e, pl.ds(pl.multiple_of(row * q, q), q), :]
        return pltpu.make_async_remote_copy(
            src_ref=block,
            dst_ref=block,
            send_sem=gather_send.at[sec, e, k - 1],
            recv_sem=gather_recv.at[sec, e, k - 1],
            device_id={"row": lax.rem(row + k, n_row)},
            device_id_type=MESH,
        )

    def start_gather(sec, e):
        for k in range(1, n_row):
            gather_copy(sec, e, k).start()

    def relay_copy(sec, e, d):
        return pltpu.make_async_remote_copy(
            src_ref=part.at[sec, e, d],
            dst_ref=relay.at[sec, e, d],
            send_sem=relay_send.at[sec, e, d],
            recv_sem=relay_recv.at[sec, e, d],
            device_id={"col": jnp.where(lower_half, 1, n_col - 2)},
            device_id_type=MESH,
        )

    def inbox_copy(sec, e, d, source):
        return pltpu.make_async_remote_copy(
            src_ref=part.at[sec, e, d],
            dst_ref=inbox.at[sec, e, source],
            send_sem=inbox_send.at[sec, e, d],
            recv_sem=inbox_recv.at[sec, e, source],
            device_id={"col": d},
            device_id_type=MESH,
        )

    def target(i):
        return jnp.where(lower_half, n_col - 1 - i, i)

    for which in range(4):
        load(which, 0).wait()
    deficit_step(0, 0, s0[0], v0[0])

    pl.semaphore_wait(barrier, n_row - 1 + n_col - 1)

    start_gather(0, 0)

    @pl.loop(1, chunks)
    def _(e):
        for which in range(4):
            load(which, e).wait()
        deficit_step(0, e, s0[e], v0[e])
        start_gather(0, e)

    for which in range(3):
        load_op(which).wait()

    rank_at = lax.broadcasted_iota(jnp.int32, (rank_max, sub), 0)
    lane_at = lax.broadcasted_iota(jnp.int32, (sub, sub), 1)

    @pl.loop(0, subs)
    def _(i):
        rows = pl.ds(pl.multiple_of(i * sub, sub), sub)
        for j in range(subs):
            far = admissible[i, j]
            live = rank_at < far * ranks[i, j]
            factor = jnp.where(live, left[i, j].astype(F32), 0.0).astype(BF16)
            low = lax.dot_general(
                factor, right[i, j], (((0,), (0,)), ((), ())), preferred_element_type=F32
            )
            near = jnp.where(
                lane_at >= far * sub, kern[rows, pl.ds(j * sub, sub)].astype(F32), low
            )
            dense[rows, pl.ds(j * sub, sub)] = near.astype(BF16)

    def multiply(sec, e):
        for k in range(1, n_row):
            gather_copy(sec, e, k).wait_recv()
        slips = slip_all[sec, e]

        @pl.loop(0, n_col)
        def _(i):
            d = target(i)
            rows = pl.ds(pl.multiple_of(d * q, q), q)
            part[sec, e, d] = jnp.dot(
                dense[rows, :], slips, preferred_element_type=F32
            ).astype(BF16)

            @pl.when(at_end & (d != col))
            def _():
                relay_copy(sec, e, d).start()

            @pl.when((~at_end) & (d != col) & ((~beside_end) | (d == end)))
            def _():
                inbox_copy(sec, e, d, col).start()

    def forward(sec, e):
        @pl.loop(0, n_col)
        def _(i):
            d = target(i)

            @pl.when(beside_end & (d != col) & (d != end))
            def _():
                relay_copy(sec, e, d).wait_recv()
                part[sec, e, d] = (
                    part[sec, e, d].astype(F32) + relay[sec, e, d].astype(F32)
                ).astype(BF16)
                inbox_copy(sec, e, d, col).start()

    def store(which, e):
        src = (out_stress, out_state, out_mean)[which]
        dst = (stress_hbm, state_hbm, mean_hbm)[which]
        return pltpu.make_async_copy(
            src.at[e], dst.at[:, pl.ds(e * LANES, LANES)], out_sem.at[which, e]
        )

    def finish(sec, e):
        total[...] = part[sec, e, col].astype(F32)

        @pl.when(beside_end)
        def _():
            relay_copy(sec, e, col).wait_recv()
            total[...] += relay[sec, e, col].astype(F32)

        @pl.loop(1, n_col - 1)
        def _(source):
            @pl.when(source != col)
            def _():
                inbox_copy(sec, e, col, source).wait_recv()
                total[...] += inbox[sec, e, source].astype(F32)

        @pl.when(sec == 0)
        def _():
            rate = total[...]
            first_stress[e] = rate
            deficit_step(
                1, e, s0[e] + time_step * rate, v0[e] + time_step * state_rate[0, e]
            )
            start_gather(1, e)

        @pl.when(sec == 1)
        def _():
            mean = 0.5 * (first_stress[e] + total[...])
            out_mean[e] = mean
            out_stress[e] = s0[e] + time_step * mean
            out_state[e] = v0[e] + 0.5 * time_step * (state_rate[0, e] + state_rate[1, e])
            for which in range(3):
                store(which, e).start()

    @pl.loop(0, steps + LAG_FINAL)
    def _(t):
        @pl.when(t < steps)
        def _():
            multiply(t // chunks, lax.rem(t, chunks))

        u = t - LAG_FORWARD

        @pl.when((u >= 0) & (u < steps))
        def _():
            forward(u // chunks, lax.rem(u, chunks))

        w = t - LAG_FINAL

        @pl.when(w >= 0)
        def _():
            finish(w // chunks, lax.rem(w, chunks))

    @pl.loop(0, steps)
    def _(t):
        sec, e = t // chunks, lax.rem(t, chunks)
        for k in range(1, n_row):
            gather_copy(sec, e, k).wait_send()

        @pl.loop(0, n_col)
        def _(d):
            @pl.when(at_end & (d != col))
            def _():
                relay_copy(sec, e, d).wait_send()

            @pl.when((~at_end) & (d != col))
            def _():
                inbox_copy(sec, e, d, col).wait_send()

    @pl.loop(0, chunks)
    def _(e):
        for which in range(3):
            store(which, e).wait()


def per_device(
    n_row,
    n_col,
    shear_stress,
    slip_state,
    friction_a,
    friction_b,
    kernel,
    left_factors,
    right_factors,
    admissible,
    ranks,
):
    q, members = shear_stress.shape
    block = kernel.shape[0]
    chunks = members // LANES
    field = pltpu.VMEM((chunks, q, LANES), F32)
    sem = pltpu.SemaphoreType.DMA
    anywhere = pl.BlockSpec(memory_space=pl.ANY)
    scalars = pl.BlockSpec(memory_space=pltpu.SMEM)
    out = jax.ShapeDtypeStruct((q, members), F32)
    return tuple(
        pl.pallas_call(
            functools.partial(step_kernel, n_row, n_col),
            out_shape=(out, out, out),
            in_specs=[anywhere] * 7 + [scalars] * 2,
            out_specs=(anywhere,) * 3,
            scratch_shapes=[
                field,
                field,
                field,
                field,
                pltpu.VMEM(kernel.shape, BF16),
                pltpu.VMEM(left_factors.shape, BF16),
                pltpu.VMEM(right_factors.shape, BF16),
                pltpu.VMEM(kernel.shape, BF16),
                pltpu.VMEM((2, chunks, q, LANES), F32),
                field,
                field,
                pltpu.VMEM((q, LANES), F32),
                pltpu.VMEM((2, chunks, n_row * q, LANES), BF16),
                pltpu.VMEM((2, chunks, n_col, q, LANES), BF16),
                pltpu.VMEM((2, chunks, n_col, q, LANES), BF16),
                pltpu.VMEM((2, chunks, n_col, q, LANES), BF16),
                field,
                field,
                field,
                sem((4, chunks)),
                sem((3,)),
                sem((3, chunks)),
                sem((2, chunks, n_row - 1)),
                sem((2, chunks, n_row - 1)),
                sem((2, chunks, n_col)),
                sem((2, chunks, n_col)),
                sem((2, chunks, n_col)),
                sem((2, chunks, n_col)),
            ],
            compiler_params=pltpu.CompilerParams(
                collective_id=0, has_side_effects=True, vmem_limit_bytes=62 * 1024 * 1024
            ),
            cost_estimate=pl.CostEstimate(
                flops=4 * block * block * members,
                bytes_accessed=7 * 4 * q * members + 2 * block * block,
                transcendentals=8 * q * members,
            ),
        )(
            shear_stress,
            slip_state,
            friction_a,
            friction_b,
            kernel,
            left_factors,
            right_factors,
            admissible,
            ranks,
        )
    )


def solution(mesh):
    vector = P(("groups", "row", "col"), None)
    return jax.shard_map(
        functools.partial(per_device, mesh.shape["row"], mesh.shape["col"]),
        mesh=mesh,
        in_specs=(
            vector,
            vector,
            vector,
            vector,
            P(("groups", "row"), "col"),
            P(("groups", "row"), "col", None, None),
            P(("groups", "row"), "col", None, None),
            P(("groups", "row"), "col"),
            P(("groups", "row"), "col"),
        ),
        out_specs=(vector, vector, vector),
        check_vma=False,
    )
```

```python
import functools

import jax
import jax.numpy as jnp
from jax import lax
from jax.experimental import pallas as pl
from jax.experimental.pallas import tpu as pltpu
from jax.sharding import PartitionSpec as P

time_step = 0.005
LANES = 128
LAG_FORWARD = 1
LAG_FINAL = 2
MESH = pl.DeviceIdType.MESH
F32 = jnp.float32
BF16 = jnp.bfloat16


def step_kernel(
    n_row,
    n_col,
    shear_hbm,
    slip_hbm,
    fa_hbm,
    fb_hbm,
    kernel_hbm,
    left_hbm,
    right_hbm,
    admissible,
    ranks,
    stress_hbm,
    state_hbm,
    s0,
    v0,
    fa,
    fb,
    kern,
    left,
    right,
    dense,
    state_rate,
    first_stress,
    first_state,
    total,
    slip_all,
    part,
    relay,
    inbox,
    out_stress,
    out_state,
    in_sem,
    op_sem,
    out_sem,
    gather_send,
    gather_recv,
    relay_send,
    relay_recv,
    inbox_send,
    inbox_recv,
):
    row = lax.axis_index("row")
    col = lax.axis_index("col")
    chunks, q = s0.shape[0], s0.shape[1]
    steps = 2 * chunks
    subs = admissible.shape[0]
    sub = left.shape[3]
    rank_max = left.shape[2]
    lower_half = col < n_col // 2
    at_end = (col == 0) | (col == n_col - 1)
    beside_end = (col == 1) | (col == n_col - 2)
    end = jnp.where(lower_half, 0, n_col - 1)

    def load(which, e):
        src = (shear_hbm, slip_hbm, fa_hbm, fb_hbm)[which]
        dst = (s0, v0, fa, fb)[which]
        return pltpu.make_async_copy(
            src.at[:, pl.ds(e * LANES, LANES)], dst.at[e], in_sem.at[which, e]
        )

    def load_op(which):
        src = (kernel_hbm, left_hbm, right_hbm)[which]
        dst = (kern, left, right)[which]
        return pltpu.make_async_copy(src, dst, op_sem.at[which])

    barrier = pltpu.get_barrier_semaphore()
    for k in range(1, n_row):
        pl.semaphore_signal(
            barrier, inc=1, device_id={"row": lax.rem(row + k, n_row)}, device_id_type=MESH
        )

    for k in range(1, n_col):
        pl.semaphore_signal(
            barrier, inc=1, device_id={"col": lax.rem(col + k, n_col)}, device_id_type=MESH
        )

    for e in range(chunks):
        for which in range(4):
            load(which, e).start()
        if e == 0:
            for which in range(3):
                load_op(which).start()

    def deficit_step(sec, e, stress, state):
        a, b = fa[e], fb[e]
        inv_a = 1.0 / a
        speed = jnp.exp((stress - state) * inv_a) - jnp.exp((-stress - state) * inv_a)
        slip_all[sec, e, pl.ds(pl.multiple_of(row * q, q), q), :] = (1.0 - speed).astype(BF16)
        state_rate[sec, e] = b * (jnp.exp(-state / b) - speed)

    def gather_copy(sec, e, k):
        block = slip_all.at[sec, e, pl.ds(pl.multiple_of(row * q, q), q), :]
        return pltpu.make_async_remote_copy(
            src_ref=block,
            dst_ref=block,
            send_sem=gather_send.at[sec, e, k - 1],
            recv_sem=gather_recv.at[sec, e, k - 1],
            device_id={"row": lax.rem(row + k, n_row)},
            device_id_type=MESH,
        )

    def start_gather(sec, e):
        for k in range(1, n_row):
            gather_copy(sec, e, k).start()

    def relay_copy(sec, e, d):
        return pltpu.make_async_remote_copy(
            src_ref=part.at[sec, e, d],
            dst_ref=relay.at[sec, e, d],
            send_sem=relay_send.at[sec, e, d],
            recv_sem=relay_recv.at[sec, e, d],
            device_id={"col": jnp.where(lower_half, 1, n_col - 2)},
            device_id_type=MESH,
        )

    def inbox_copy(sec, e, d, source):
        return pltpu.make_async_remote_copy(
            src_ref=part.at[sec, e, d],
            dst_ref=inbox.at[sec, e, source],
            send_sem=inbox_send.at[sec, e, d],
            recv_sem=inbox_recv.at[sec, e, source],
            device_id={"col": d},
            device_id_type=MESH,
        )

    def target(i):
        return jnp.where(lower_half, n_col - 1 - i, i)

    for which in range(4):
        load(which, 0).wait()
    deficit_step(0, 0, s0[0], v0[0])

    pl.semaphore_wait(barrier, n_row - 1 + n_col - 1)

    start_gather(0, 0)

    @pl.loop(1, chunks)
    def _(e):
        for which in range(4):
            load(which, e).wait()
        deficit_step(0, e, s0[e], v0[e])
        start_gather(0, e)

    for which in range(3):
        load_op(which).wait()

    rank_at = lax.broadcasted_iota(jnp.int32, (rank_max, sub), 0)
    lane_at = lax.broadcasted_iota(jnp.int32, (sub, sub), 1)

    @pl.loop(0, subs)
    def _(i):
        rows = pl.ds(pl.multiple_of(i * sub, sub), sub)
        for j in range(subs):
            far = admissible[i, j]
            live = rank_at < far * ranks[i, j]
            factor = jnp.where(live, left[i, j].astype(F32), 0.0).astype(BF16)
            low = lax.dot_general(
                factor, right[i, j], (((0,), (0,)), ((), ())), preferred_element_type=F32
            )
            near = jnp.where(
                lane_at >= far * sub, kern[rows, pl.ds(j * sub, sub)].astype(F32), low
            )
            dense[rows, pl.ds(j * sub, sub)] = near.astype(BF16)

    def multiply(sec, e):
        for k in range(1, n_row):
            gather_copy(sec, e, k).wait_recv()
        slips = slip_all[sec, e]

        @pl.loop(0, n_col)
        def _(i):
            d = target(i)
            rows = pl.ds(pl.multiple_of(d * q, q), q)
            part[sec, e, d] = jnp.dot(
                dense[rows, :], slips, preferred_element_type=F32
            ).astype(BF16)

            @pl.when(at_end & (d != col))
            def _():
                relay_copy(sec, e, d).start()

            @pl.when((~at_end) & (d != col) & ((~beside_end) | (d == end)))
            def _():
                inbox_copy(sec, e, d, col).start()

    def forward(sec, e):
        @pl.loop(0, n_col)
        def _(i):
            d = target(i)

            @pl.when(beside_end & (d != col) & (d != end))
            def _():
                relay_copy(sec, e, d).wait_recv()
                part[sec, e, d] = (
                    part[sec, e, d].astype(F32) + relay[sec, e, d].astype(F32)
                ).astype(BF16)
                inbox_copy(sec, e, d, col).start()

    def store(which, e):
        src = (out_stress, out_state)[which]
        dst = (stress_hbm, state_hbm)[which]
        return pltpu.make_async_copy(
            src.at[e], dst.at[:, pl.ds(e * LANES, LANES)], out_sem.at[which, e]
        )

    def finish(sec, e):
        total[...] = part[sec, e, col].astype(F32)

        @pl.when(beside_end)
        def _():
            relay_copy(sec, e, col).wait_recv()
            total[...] += relay[sec, e, col].astype(F32)

        @pl.loop(1, n_col - 1)
        def _(source):
            @pl.when(source != col)
            def _():
                inbox_copy(sec, e, col, source).wait_recv()
                total[...] += inbox[sec, e, source].astype(F32)

        @pl.when(sec == 0)
        def _():
            rate = total[...]
            first_stress[e] = rate
            deficit_step(
                1, e, s0[e] + time_step * rate, v0[e] + time_step * state_rate[0, e]
            )
            start_gather(1, e)

        @pl.when(sec == 1)
        def _():
            out_stress[e] = first_stress[e] + total[...]
            out_state[e] = state_rate[0, e] + state_rate[1, e]
            for which in range(2):
                store(which, e).start()

    @pl.loop(0, steps + LAG_FINAL)
    def _(t):
        @pl.when(t < steps)
        def _():
            multiply(t // chunks, lax.rem(t, chunks))

        u = t - LAG_FORWARD

        @pl.when((u >= 0) & (u < steps))
        def _():
            forward(u // chunks, lax.rem(u, chunks))

        w = t - LAG_FINAL

        @pl.when(w >= 0)
        def _():
            finish(w // chunks, lax.rem(w, chunks))

    @pl.loop(0, steps)
    def _(t):
        sec, e = t // chunks, lax.rem(t, chunks)
        for k in range(1, n_row):
            gather_copy(sec, e, k).wait_send()

        @pl.loop(0, n_col)
        def _(d):
            @pl.when(at_end & (d != col))
            def _():
                relay_copy(sec, e, d).wait_send()

            @pl.when((~at_end) & (d != col))
            def _():
                inbox_copy(sec, e, d, col).wait_send()

    @pl.loop(0, chunks)
    def _(e):
        for which in range(2):
            store(which, e).wait()


def per_device(
    n_row,
    n_col,
    shear_stress,
    slip_state,
    friction_a,
    friction_b,
    kernel,
    left_factors,
    right_factors,
    admissible,
    ranks,
):
    q, members = shear_stress.shape
    block = kernel.shape[0]
    chunks = members // LANES
    field = pltpu.VMEM((chunks, q, LANES), F32)
    sem = pltpu.SemaphoreType.DMA
    anywhere = pl.BlockSpec(memory_space=pl.ANY)
    scalars = pl.BlockSpec(memory_space=pltpu.SMEM)
    out = jax.ShapeDtypeStruct((q, members), F32)
    stress_sum, state_sum = (
        pl.pallas_call(
            functools.partial(step_kernel, n_row, n_col),
            out_shape=(out, out),
            in_specs=[anywhere] * 7 + [scalars] * 2,
            out_specs=(anywhere,) * 2,
            scratch_shapes=[
                field,
                field,
                field,
                field,
                pltpu.VMEM(kernel.shape, BF16),
                pltpu.VMEM(left_factors.shape, BF16),
                pltpu.VMEM(right_factors.shape, BF16),
                pltpu.VMEM(kernel.shape, BF16),
                pltpu.VMEM((2, chunks, q, LANES), F32),
                field,
                field,
                pltpu.VMEM((q, LANES), F32),
                pltpu.VMEM((2, chunks, n_row * q, LANES), BF16),
                pltpu.VMEM((2, chunks, n_col, q, LANES), BF16),
                pltpu.VMEM((2, chunks, n_col, q, LANES), BF16),
                pltpu.VMEM((2, chunks, n_col, q, LANES), BF16),
                field,
                field,
                sem((4, chunks)),
                sem((3,)),
                sem((2, chunks)),
                sem((2, chunks, n_row - 1)),
                sem((2, chunks, n_row - 1)),
                sem((2, chunks, n_col)),
                sem((2, chunks, n_col)),
                sem((2, chunks, n_col)),
                sem((2, chunks, n_col)),
            ],
            compiler_params=pltpu.CompilerParams(
                collective_id=0, has_side_effects=True, vmem_limit_bytes=62 * 1024 * 1024
            ),
            cost_estimate=pl.CostEstimate(
                flops=4 * block * block * members,
                bytes_accessed=7 * 4 * q * members + 2 * block * block,
                transcendentals=8 * q * members,
            ),
        )(
            shear_stress,
            slip_state,
            friction_a,
            friction_b,
            kernel,
            left_factors,
            right_factors,
            admissible,
            ranks,
        )
    )
    mean_rate = 0.5 * stress_sum
    new_stress = shear_stress + time_step * mean_rate
    new_state = slip_state + 0.5 * time_step * state_sum
    return new_stress, new_state, mean_rate


def solution(mesh):
    vector = P(("groups", "row", "col"), None)
    return jax.shard_map(
        functools.partial(per_device, mesh.shape["row"], mesh.shape["col"]),
        mesh=mesh,
        in_specs=(
            vector,
            vector,
            vector,
            vector,
            P(("groups", "row"), "col"),
            P(("groups", "row"), "col", None, None),
            P(("groups", "row"), "col", None, None),
            P(("groups", "row"), "col"),
            P(("groups", "row"), "col"),
        ),
        out_specs=(vector, vector, vector),
        check_vma=False,
    )
```
